512 devices in a mesh: row: 32 (over z, x_lo), col: 16 (over y, x_hi, core).
Axes of the slice: x: 4 (x_hi: 2, x_lo: 2; x = x_hi * 2 + x_lo), y: 4, z: 16, core: 2. Of those that a mesh axis runs over, the one named last changes fastest.
Arguments:
- samples: bfloat16 [32, 262144], P('row', 'col'), may hold values from -6 to 6
- blocks: bfloat16 [32, 16, 32, 128, 128], P('row', 'col'), may hold values from -0.29882812 to 0.29882812
- diagonal: float32 [262144], P('col'), may hold values from 0.5 to 2
- block_rows: int32 [32, 16, 32], P('row', 'col'), may hold values from 0 to 63, as said below
- block_cols: int32 [32, 16, 32], P('row', 'col'), may hold values from 0 to 127, as said below
Outputs:
- new_blocks: bfloat16 [32, 16, 32, 128, 128], P('row', 'col')
- new_diagonal: float32 [262144], P('col')
The draws below stay inside these ranges and needn't reach their ends.
Inputs may be any that keep to these rules, and one draw needn't show every extreme that they name: Within a grid cell the 32 pairs (block_rows, block_cols) are distinct. `block_cols`: pairs with block_rows, as stated there.
All inputs are finite; a program needn't handle non-finite values.
Results may differ from the reference program's by a relative error of at most 0.018.
Values may be sent and summed in bfloat16 or wider, within the bound.
No kernel may reach another device: no remote copies, remote signals or barrier semaphores. Data moves between devices by JAX's collectives and lax.ppermute only.
A program may use at most 64 MiB of HBM per device.

```python
import math
import jax
import jax.numpy as jnp
from jax import lax

B = 128
BLK = 2048
K = 32
NS = 32
P_SIZE = 262144
RB = 64
CB = 128
N_ROW = 32
N_COL = 16


def positions(key):
    keys = jax.random.split(key, N_ROW * N_COL)
    picked = jax.vmap(lambda single: jax.random.permutation(single, RB * CB)[:K])(keys)
    return picked.reshape(N_ROW, N_COL, K).astype(jnp.int32)


def draw_block_rows(key, part):
    shared = positions(key)
    return shared // CB


def draw_block_cols(key, part):
    shared = positions(key)
    return shared % CB


def level_of(stream_key, extent, pieces, smallest, high):
    loudness, own = 1.0, jax.random.fold_in(stream_key, 6)
    for position, blocks in pieces:
        heights = jnp.exp(jax.random.uniform(jax.random.fold_in(own, position), (blocks,), jnp.float32, smallest / len(pieces), high / len(pieces)))
        loudness = loudness * jnp.repeat(heights, extent[position] // blocks).reshape([-1 if axis == position else 1 for axis in range(len(extent))])
    return loudness


def gaussian(stream_key, shape, deviation, limit, pieces=(), held_as=jnp.bfloat16):
    array = jax.random.normal(stream_key, shape, jnp.float32) * deviation
    if len(pieces) > 0:
        array = level_of(stream_key, shape, pieces, -0.22, 0.18) * array
    return jnp.clip(array, min=-limit, max=limit).astype(held_as)


def setup_inputs(seed: int = 0) -> dict:
    key_list = jax.random.split(jax.random.key(seed), 6)
    samples = gaussian(key_list[0], (NS, P_SIZE), 1.0, 6.0, ((0, 32), (1, 16)))
    blocks = gaussian(key_list[1], (N_ROW, N_COL, K, B, B), 0.05, 0.29882812, ((0, 32), (1, 16)))
    diagonal = jnp.clip(jnp.exp(math.log(2.0) - 1.3862944 * jax.random.uniform(key_list[2], (P_SIZE,), jnp.float32) ** level_of(key_list[2], (P_SIZE,), ((0, 16),), -0.2, 0.2)), 0.5, 2.0)
    block_rows = draw_block_rows(jax.random.fold_in(key_list[5], 71), 0)
    block_cols = draw_block_cols(jax.random.fold_in(key_list[5], 71), 0)
    return {"samples": samples, "blocks": blocks, "diagonal": diagonal, "block_rows": block_rows, "block_cols": block_cols}


TAU = 0.5
PENALTY = 0.1


def reference(samples, blocks, diagonal, block_rows, block_cols):
    count = samples.shape[0]
    xblocks = samples.reshape(count, BLK, B)
    rows_g = block_rows + (RB * jnp.arange(N_ROW, dtype=jnp.int32))[:, None, None]
    cols_g = block_cols + (CB * jnp.arange(N_COL, dtype=jnp.int32))[None, :, None]

    def add_group(carry, index):
        gathered = xblocks[:, rows_g[index]].astype(jnp.float32)
        prod = jnp.einsum('nckb,ckbj->cknj', gathered, blocks[index].astype(jnp.float32))
        summed = jax.ops.segment_sum(prod.reshape(N_COL * K, count, B), cols_g[index].reshape(-1), num_segments=BLK)
        rounded = lax.optimization_barrier(summed.astype(jnp.bfloat16)).astype(jnp.float32)
        return carry + rounded, None

    total, _ = lax.scan(add_group, jnp.zeros((BLK, count, B), jnp.float32), jnp.arange(N_ROW, dtype=jnp.int32))
    total = jnp.transpose(total, (1, 0, 2)).reshape(count, P_SIZE)
    mixed = (total + samples.astype(jnp.float32) * diagonal[None, :]).astype(jnp.bfloat16)
    quad = jnp.einsum('np,np->p', samples.astype(jnp.float32), mixed.astype(jnp.float32))
    diag_grad = -1.0 / diagonal + quad / count
    new_diagonal = diagonal - TAU * diag_grad
    mblocks = mixed.reshape(count, BLK, B)

    def update(index):
        xr = xblocks[:, rows_g[index]].astype(jnp.float32)
        wc = mblocks[:, cols_g[index]].astype(jnp.float32)
        xc = xblocks[:, cols_g[index]].astype(jnp.float32)
        wr = mblocks[:, rows_g[index]].astype(jnp.float32)
        direct = jnp.einsum('ncki,nckj->ckij', xr, wc) / count
        partner = jnp.einsum('ncki,nckj->ckij', xc, wr) / count
        grad = 0.5 * (direct + jnp.swapaxes(partner, -1, -2))
        moved = blocks[index].astype(jnp.float32) - TAU * grad
        shrunk = jnp.sign(moved) * jnp.maximum(jnp.abs(moved) - TAU * PENALTY, 0.0)
        return shrunk.astype(jnp.bfloat16)

    new_blocks = lax.map(update, jnp.arange(N_ROW, dtype=jnp.int32))
    return new_blocks, new_diagonal
```

```python
import jax
import jax.numpy as jnp
from jax import lax
from jax.sharding import PartitionSpec as P

TAU = 0.5
PENALTY = 0.1
BF = jnp.bfloat16


def exchange(x, axis):
    return lax.all_to_all(x, axis, 0, 0, tiled=True)


def spread(x, axis):
    return exchange(jnp.broadcast_to(x[None], (lax.axis_size(axis),) + x.shape), axis)


def pick(index, size):
    return (index.reshape(-1, 1) == jnp.arange(size, dtype=index.dtype)[None, :]).astype(BF)


def turned(x, nrow, ncol):
    ratio = nrow // ncol
    rindex = lax.axis_index("row")
    mine = rindex % ratio
    parts = x.reshape((ratio, -1) + x.shape[1:])
    got = []
    for shift in range(ratio):
        target = (mine + shift) % ratio
        part = lax.dynamic_index_in_dim(parts, target, 0, keepdims=False)
        perm = []
        for r in range(nrow):
            for c in range(ncol):
                to = c * ratio + (r + shift) % ratio
                perm.append((r * ncol + c, to * ncol + r // ratio))
        got.append(lax.ppermute(part, ("row", "col"), perm))
    out = []
    for e in range(ratio):
        value = got[0]
        for shift in range(1, ratio):
            value = jnp.where((mine - shift) % ratio == e, got[shift], value)
        out.append(value)
    return jnp.concatenate(out, axis=1)


def on_device(samples, blocks, diagonal, block_rows, block_cols):
    nrow, ncol = lax.axis_size("row"), lax.axis_size("col")
    ratio = nrow // ncol
    width = samples.shape[1]
    b = blocks.shape[-1]
    cb = width // b
    rb = cb // ratio
    rows, cols, local = block_rows[0, 0], block_cols[0, 0], blocks[0, 0]
    k = rows.shape[0]
    x = samples.reshape(cb, b)
    diag = diagonal.reshape(cb, b)

    pick_r = pick(spread(rows[None], "col"), rb)
    pick_c = pick(spread(cols[None], "row"), cb)

    def to_rows(v):
        t = turned(v, nrow, ncol)
        out = jnp.dot(pick_r, t, preferred_element_type=jnp.float32).astype(BF)
        got = exchange(out.reshape(ncol, k, ratio * b), "col")
        return got.reshape(ncol, k, ratio, b).transpose(0, 2, 1, 3).reshape(nrow, k, b)

    def to_cols(v):
        out = jnp.dot(pick_c, v, preferred_element_type=jnp.float32).astype(BF)
        return exchange(out.reshape(nrow, k, b), "row")

    xr = to_rows(x)
    xc = to_cols(x)
    prod = jnp.einsum("nki,kij->nkj", xr, local, preferred_element_type=jnp.float32)
    terms = exchange(prod.astype(BF), "row").reshape(nrow * k, b)
    total = lax.dot_general(pick_c, terms, (((0,), (0,)), ((), ())), preferred_element_type=jnp.float32)
    xf = x.astype(jnp.float32)
    mixed = (total + xf * diag).astype(BF)

    quads = exchange((xf * mixed.astype(jnp.float32)).reshape(nrow, cb // nrow, b), "row")
    quad = jnp.sum(quads, axis=0)
    mine = lax.dynamic_index_in_dim(diag.reshape(nrow, cb // nrow, b), lax.axis_index("row"), 0, keepdims=False)
    diag_grad = -1.0 / mine + quad / nrow
    new_diagonal = spread(mine - TAU * diag_grad, "row").reshape(width)

    wr = to_rows(mixed)
    wc = to_cols(mixed)
    left = jnp.concatenate([xr, wr], axis=0)
    right = jnp.concatenate([wc, xc], axis=0)
    both = jnp.einsum("nki,nkj->kij", left, right, preferred_element_type=jnp.float32)
    grad = both * (0.5 / nrow)
    moved = local.astype(jnp.float32) - TAU * grad
    shrunk = jnp.sign(moved) * jnp.maximum(jnp.abs(moved) - TAU * PENALTY, 0.0)
    return shrunk.astype(BF)[None, None], new_diagonal


def solution(mesh):
    in_specs = (
        P("row", "col"),
        P("row", "col", None, None, None),
        P("col"),
        P("row", "col", None),
        P("row", "col", None),
    )
    out_specs = (P("row", "col", None, None, None), P("col"))
    return jax.shard_map(
        on_device, mesh=mesh, in_specs=in_specs, out_specs=out_specs, check_vma=False
    )
```

```python
import jax
import jax.numpy as jnp
from jax import lax
from jax.sharding import PartitionSpec as P

TAU = 0.5
PENALTY = 0.1
BF = jnp.bfloat16


def exchange(x, axis):
    return lax.all_to_all(x, axis, 0, 0, tiled=True)


def spread(x, axis):
    return exchange(jnp.broadcast_to(x[None], (lax.axis_size(axis),) + x.shape), axis)


def pick(index, size):
    return (index.reshape(-1, 1) == jnp.arange(size, dtype=index.dtype)[None, :]).astype(BF)


def turned(x, nrow, ncol):
    ratio = nrow // ncol
    rindex = lax.axis_index("row")
    mine = rindex % ratio
    parts = x.reshape((ratio, -1) + x.shape[1:])
    got = []
    for shift in range(ratio):
        target = (mine + shift) % ratio
        part = lax.dynamic_index_in_dim(parts, target, 0, keepdims=False)
        perm = []
        for r in range(nrow):
            for c in range(ncol):
                to = c * ratio + (r + shift) % ratio
                perm.append((r * ncol + c, to * ncol + r // ratio))
        got.append(lax.ppermute(part, ("row", "col"), perm))
    out = []
    for e in range(ratio):
        value = got[0]
        for shift in range(1, ratio):
            value = jnp.where((mine - shift) % ratio == e, got[shift], value)
        out.append(value)
    return jnp.concatenate(out, axis=1)


def halves(v):
    high = lax.reduce_precision(v, 8, 7)
    return high.astype(BF), (v - high).astype(BF)


def on_device(samples, blocks, diagonal, block_rows, block_cols):
    nrow, ncol = lax.axis_size("row"), lax.axis_size("col")
    rindex = lax.axis_index("row")
    ratio = nrow // ncol
    width = samples.shape[1]
    b = blocks.shape[-1]
    cb = width // b
    rb = cb // ratio
    own = cb // nrow
    rows, cols, local = block_rows[0, 0], block_cols[0, 0], blocks[0, 0]
    k = rows.shape[0]
    x = samples.reshape(cb, b)
    diag = diagonal.reshape(cb, b)

    def by_sample(got):
        return got.reshape(ncol, k, ratio, b).transpose(0, 2, 1, 3).reshape(nrow, k, b)

    xt = turned(x, nrow, ncol)
    tail = jnp.zeros((8, ratio * b), BF).at[0, :k].set(rows.astype(BF))
    got = spread(jnp.concatenate([xt, tail])[None], "col").reshape(ncol, rb + 8, ratio * b)
    pick_r = pick(got[:, rb, :k].astype(jnp.int32), rb)
    pick_own = pick(rows, rb + 8)
    xr = by_sample(jnp.einsum("sb,dbl->dsl", pick_own, got, preferred_element_type=jnp.float32).astype(BF))

    prod = jnp.einsum("nki,kij->nkj", xr, local, preferred_element_type=jnp.float32).astype(BF)
    tail = jnp.zeros((8, b), BF).at[0, :k].set(cols.astype(BF))
    got = exchange(jnp.concatenate([prod, jnp.broadcast_to(tail[None], (nrow, 8, b))], axis=1), "row")
    named = jnp.pad(got[:, k, :k].astype(jnp.int32), ((0, 0), (0, 8)), constant_values=-1)
    pick_c = pick(named, cb)
    total = lax.dot_general(
        pick_c, got.reshape(nrow * (k + 8), b), (((0,), (0,)), ((), ())), preferred_element_type=jnp.float32
    )
    mixed = (total + x.astype(jnp.float32) * diag).astype(BF)

    mt = turned(mixed, nrow, ncol)
    wr = jnp.dot(pick_r, mt, preferred_element_type=jnp.float32).astype(BF).reshape(ncol, k, ratio * b)
    both = xt.astype(jnp.float32) * mt.astype(jnp.float32)
    quad = jnp.sum(both.reshape(rb, ratio, b), axis=1).reshape(ncol, own, b)
    tail = jnp.pad(jnp.concatenate(halves(quad), axis=2), ((0, 0), (0, 8 - own), (0, 0)))
    got = exchange(jnp.concatenate([wr, tail], axis=1), "col")
    wr = by_sample(got[:, :k])
    quad = jnp.sum(got[:, k : k + own].astype(jnp.float32), axis=0)
    quad = quad[:, :b] + quad[:, b:]
    perm = []
    for r in range(nrow):
        for c in range(ncol):
            perm.append((r * ncol + c, (r % ratio * ncol + c) * ncol + r // ratio))
    quad = lax.ppermute(quad, ("row", "col"), perm)
    mine = lax.dynamic_slice_in_dim(diag, rindex * own, own, 0)
    diag_grad = -1.0 / mine + quad / nrow
    tail = jnp.concatenate(halves(mine - TAU * diag_grad), axis=0)

    out = jnp.dot(pick_c, jnp.concatenate([mixed, x], axis=1), preferred_element_type=jnp.float32).astype(BF)
    out = out.reshape(nrow, k + 8, 2 * b)[:, :k]
    out = jnp.concatenate([out[..., :b], jnp.broadcast_to(tail[None], (nrow, 8, b)), out[..., b:]], axis=1)
    got = exchange(out, "row")
    wc, xc = got[:, :k], got[:, k + 8 :]
    new_diagonal = got[:, k : k + own].astype(jnp.float32) + got[:, k + own : k + 2 * own].astype(jnp.float32)

    left = jnp.concatenate([xr, wr], axis=0)
    right = jnp.concatenate([wc, xc], axis=0)
    both = jnp.einsum("nki,nkj->kij", left, right, preferred_element_type=jnp.float32)
    grad = both * (0.5 / nrow)
    moved = local.astype(jnp.float32) - TAU * grad
    shrunk = jnp.sign(moved) * jnp.maximum(jnp.abs(moved) - TAU * PENALTY, 0.0)
    return shrunk.astype(BF)[None, None], new_diagonal.reshape(width)


def solution(mesh):
    in_specs = (
        P("row", "col"),
        P("row", "col", None, None, None),
        P("col"),
        P("row", "col", None),
        P("row", "col", None),
    )
    out_specs = (P("row", "col", None, None, None), P("col"))
    return jax.shard_map(
        on_device, mesh=mesh, in_specs=in_specs, out_specs=out_specs, check_vma=False
    )
```

```python
import jax
import jax.numpy as jnp
from jax import lax
from jax.sharding import PartitionSpec as P

TAU = 0.5
PENALTY = 0.1
BF = jnp.bfloat16


def exchange(x, axis):
    return lax.all_to_all(x, axis, 0, 0, tiled=True)


def spread(x, axis):
    return exchange(jnp.broadcast_to(x[None], (lax.axis_size(axis),) + x.shape), axis)


def pick(index, size):
    return (index.reshape(-1, 1) == jnp.arange(size, dtype=index.dtype)[None, :]).astype(BF)


def halves(v):
    high = lax.reduce_precision(v, 8, 7)
    return high.astype(BF), (v - high).astype(BF)


def on_device(samples, blocks, diagonal, block_rows, block_cols):
    nrow, ncol = lax.axis_size("row"), lax.axis_size("col")
    ratio = nrow // ncol
    width = samples.shape[1]
    b = blocks.shape[-1]
    cb = width // b
    rb = cb // ratio
    own = cb // nrow
    rows, cols, local = block_rows[0, 0], block_cols[0, 0], blocks[0, 0]
    k = rows.shape[0]
    x = samples.reshape(cb, b)
    diag = diagonal.reshape(cb, b)

    groups = [[(ratio * g + n % ratio) * ncol + n // ratio for n in range(nrow)] for g in range(ncol)]
    perm = [(n * ncol + g, groups[g][n]) for n in range(nrow) for g in range(ncol)]

    def turned(v):
        return lax.ppermute(v, ("row", "col"), perm)

    def in_group(v):
        return lax.all_to_all(v, ("row", "col"), 0, 0, tiled=True, axis_index_groups=groups)

    tail = jnp.zeros((8, b), BF).at[0, :k].set(rows.astype(BF))
    parts = turned(x).reshape(ratio, rb, b)
    parts = jnp.concatenate([parts, jnp.broadcast_to(tail[None], (ratio, 8, b))], axis=1)
    got = in_group(jnp.broadcast_to(parts[None], (ncol, ratio, rb + 8, b)).reshape(nrow, rb + 8, b))
    named = got[:, rb, :k].astype(jnp.int32) + rb * (jnp.arange(nrow, dtype=jnp.int32) % ratio)[:, None]
    pick_r = pick(named, cb)
    xr = jnp.einsum("sb,nbl->nsl", pick(rows, rb + 8), got, preferred_element_type=jnp.float32).astype(BF)

    prod = jnp.einsum("nki,kij->nkj", xr, local, preferred_element_type=jnp.float32).astype(BF)
    tail = jnp.zeros((8, b), BF).at[0, :k].set(cols.astype(BF))
    got = exchange(jnp.concatenate([prod, jnp.broadcast_to(tail[None], (nrow, 8, b))], axis=1), "row")
    named = jnp.pad(got[:, k, :k].astype(jnp.int32), ((0, 0), (0, 8)), constant_values=-1)
    pick_c = pick(named, cb)
    total = lax.dot_general(
        pick_c, got.reshape(nrow * (k + 8), b), (((0,), (0,)), ((), ())), preferred_element_type=jnp.float32
    )
    xf = x.astype(jnp.float32)
    mixed = (total + xf * diag).astype(BF)
    mt = turned(mixed)

    quad = (xf * mixed.astype(jnp.float32)).reshape(nrow, own, b)
    out = jnp.dot(pick_c, jnp.concatenate([mixed, x], axis=1), preferred_element_type=jnp.float32).astype(BF)
    out = out.reshape(nrow, k + 8, 2 * b)[:, :k]
    got = exchange(jnp.concatenate([out[..., :b], *halves(quad), out[..., b:]], axis=1), "row")
    got, mt = lax.optimization_barrier((got, mt))
    wc, xc = got[:, :k], got[:, k + 2 * own :]
    quad = jnp.sum(got[:, k : k + 2 * own].astype(jnp.float32), axis=0)
    quad = quad[:own] + quad[own:]
    mine = lax.dynamic_slice_in_dim(diag, lax.axis_index("row") * own, own, 0)
    diag_grad = -1.0 / mine + quad / nrow
    mine = mine - TAU * diag_grad

    wr = in_group(jnp.dot(pick_r, mt, preferred_element_type=jnp.float32).astype(BF).reshape(nrow, k, b))
    wr, mine = lax.optimization_barrier((wr, mine))
    new_diagonal = spread(mine, "row").reshape(width)

    left = jnp.concatenate([xr, wr], axis=0)
    right = jnp.concatenate([wc, xc], axis=0)
    both = jnp.einsum("nki,nkj->kij", left, right, preferred_element_type=jnp.float32)
    grad = both * (0.5 / nrow)
    moved = local.astype(jnp.float32) - TAU * grad
    shrunk = jnp.sign(moved) * jnp.maximum(jnp.abs(moved) - TAU * PENALTY, 0.0)
    return shrunk.astype(BF)[None, None], new_diagonal


def solution(mesh):
    in_specs = (
        P("row", "col"),
        P("row", "col", None, None, None),
        P("col"),
        P("row", "col", None),
        P("row", "col", None),
    )
    out_specs = (P("row", "col", None, None, None), P("col"))
    return jax.shard_map(
        on_device, mesh=mesh, in_specs=in_specs, out_specs=out_specs, check_vma=False
    )
```

```python
import jax
import jax.numpy as jnp
from jax import lax
from jax.sharding import PartitionSpec as P

TAU = 0.5
PENALTY = 0.1
ORDER = (16, 4, 8, 2)
BF = jnp.bfloat16


def member_order():
    order = [0]
    for bit in (1,) + ORDER:
        order = order + [n + bit for n in order]
    return order


def exchange(x):
    return lax.all_to_all(x, "row", 0, 0, tiled=True, axis_index_groups=[member_order()])


def pick(index, size):
    return (index.reshape(-1, 1) == jnp.arange(size, dtype=index.dtype)[None, :]).astype(BF)


def halves(v):
    high = lax.reduce_precision(v, 8, 7)
    return high.astype(BF), (v - high).astype(BF)


def on_device(samples, blocks, diagonal, block_rows, block_cols):
    nrow, ncol = lax.axis_size("row"), lax.axis_size("col")
    ratio = nrow // ncol
    width = samples.shape[1]
    b = blocks.shape[-1]
    cb = width // b
    rb = cb // ratio
    own = cb // nrow
    rows, cols, local = block_rows[0, 0], block_cols[0, 0], blocks[0, 0]
    k = rows.shape[0]
    x = samples.reshape(cb, b)
    diag = diagonal.reshape(cb, b)

    order = member_order()
    groups = [[(ratio * g + n % ratio) * ncol + n // ratio for n in range(nrow)] for g in range(ncol)]
    perm = [(n * ncol + g, groups[g][n]) for n in range(nrow) for g in range(ncol)]

    def turned(v):
        return lax.ppermute(v, ("row", "col"), perm)

    def in_group(v):
        return lax.all_to_all(v, ("row", "col"), 0, 0, tiled=True, axis_index_groups=[[group[n] for n in order] for group in groups])

    me = lax.axis_index("col") * ratio + lax.axis_index("row") % ratio

    def swap(v, bit):
        pairs = [(group[n], group[n ^ bit]) for group in groups for n in range(nrow)]
        return lax.ppermute(v, ("row", "col"), pairs)

    def double(v, bit):
        upper = (me & bit) == bit
        other = swap(v, bit)
        return jnp.concatenate([jnp.where(upper, other, v), jnp.where(upper, v, other)])

    def named_rows(v):
        return jnp.einsum("sb,nbl->nsl", pick_r, v, preferred_element_type=jnp.float32).astype(BF)

    parts = turned(x).reshape(1, ratio, rb, b)
    got = in_group(jnp.broadcast_to(parts, (ncol, ratio, rb, b)).reshape(nrow, rb, b))
    pick_r = pick(rows, rb)
    xr = named_rows(got)

    prod = jnp.einsum("nki,kij->nkj", xr, local, preferred_element_type=jnp.float32).astype(BF)
    tail = jnp.zeros((8, b), BF).at[0, :k].set(cols.astype(BF))
    got = exchange(jnp.concatenate([prod, jnp.broadcast_to(tail[None], (nrow, 8, b))], axis=1))
    named = jnp.pad(got[:, k, :k].astype(jnp.int32), ((0, 0), (0, 8)), constant_values=-1)
    pick_c = pick(named, cb)
    total = lax.dot_general(
        pick_c, got.reshape(nrow * (k + 8), b), (((0,), (0,)), ((), ())), preferred_element_type=jnp.float32
    )
    xf = x.astype(jnp.float32)
    mixed = (total + xf * diag).astype(BF)

    quad = (xf * mixed.astype(jnp.float32)).reshape(nrow, own, b)
    out = jnp.dot(pick_c, jnp.concatenate([mixed, x], axis=1), preferred_element_type=jnp.float32).astype(BF)
    out = out.reshape(nrow, k + 8, 2 * b)[:, :k]
    out = jnp.concatenate([out[..., :b], *halves(quad), out[..., b:]], axis=1)
    out, mixed = lax.optimization_barrier((out, mixed))
    got = exchange(out)

    mt = turned(mixed)
    upper = (me & 1) == 1
    low, high = mt[:rb], mt[rb:]
    mine, other = jnp.where(upper, high, low), swap(jnp.where(upper, low, high), 1)
    held = jnp.where(upper, jnp.stack([other, mine]), jnp.stack([mine, other]))
    for bit in ORDER[:-1]:
        held = double(held, bit)
    held, got = lax.optimization_barrier((held, got))
    other = swap(held, ORDER[-1])
    upper = (me & ORDER[-1]) == ORDER[-1]
    held, other = named_rows(held), named_rows(other)
    wr = jnp.where(upper, jnp.concatenate([other, held]), jnp.concatenate([held, other]))

    wc, xc = got[:, :k], got[:, k + 2 * own :]
    quad = jnp.sum(got[:, k : k + 2 * own].astype(jnp.float32), axis=0)
    quad = quad[:own] + quad[own:]
    place = jnp.array([order.index(n) for n in range(nrow)], jnp.int32)[lax.axis_index("row")]
    mine = lax.dynamic_slice_in_dim(diag, place * own, own, 0)
    diag_grad = -1.0 / mine + quad / nrow
    mine = mine - TAU * diag_grad

    new_diagonal = exchange(jnp.broadcast_to(mine[None], (nrow, own, b))).reshape(width)

    left = jnp.concatenate([xr, wr], axis=0)
    right = jnp.concatenate([wc, xc], axis=0)
    both = jnp.einsum("nki,nkj->kij", left, right, preferred_element_type=jnp.float32)
    grad = both * (0.5 / nrow)
    moved = local.astype(jnp.float32) - TAU * grad
    shrunk = jnp.sign(moved) * jnp.maximum(jnp.abs(moved) - TAU * PENALTY, 0.0)
    return shrunk.astype(BF)[None, None], new_diagonal


def solution(mesh):
    in_specs = (
        P("row", "col"),
        P("row", "col", None, None, None),
        P("col"),
        P("row", "col", None),
        P("row", "col", None),
    )
    out_specs = (P("row", "col", None, None, None), P("col"))
    return jax.shard_map(
        on_device, mesh=mesh, in_specs=in_specs, out_specs=out_specs, check_vma=False
    )
```

```python
import jax
import jax.numpy as jnp
from jax import lax
from jax.sharding import PartitionSpec as P

TAU = 0.5
PENALTY = 0.1
COL_BITS = (8, 2, 4, 1)
BF = jnp.bfloat16


def member_order():
    order = [0]
    for bit in COL_BITS:
        order = order + [c + bit for c in order]
    return [2 * c + e for c in order for e in range(2)]


def exchange(x):
    return lax.all_to_all(x, "row", 0, 0, tiled=True, axis_index_groups=[member_order()])


def pick(index, size):
    return (index.reshape(-1, 1) == jnp.arange(size, dtype=index.dtype)[None, :]).astype(BF)


def halves(v):
    high = lax.reduce_precision(v, 8, 7)
    return high.astype(BF), (v - high).astype(BF)


def on_device(samples, blocks, diagonal, block_rows, block_cols):
    nrow, ncol = lax.axis_size("row"), lax.axis_size("col")
    ratio = nrow // ncol
    width = samples.shape[1]
    b = blocks.shape[-1]
    cb = width // b
    rb = cb // ratio
    own = cb // nrow
    rows, cols, local = block_rows[0, 0], block_cols[0, 0], blocks[0, 0]
    k = rows.shape[0]
    x = samples.reshape(cb, b)
    diag = diagonal.reshape(cb, b)

    order = member_order()
    groups = [[(ratio * g + n % ratio) * ncol + n // ratio for n in range(nrow)] for g in range(ncol)]
    perm = [(n * ncol + g, groups[g][n]) for n in range(nrow) for g in range(ncol)]

    def turned(v):
        return lax.ppermute(v, ("row", "col"), perm)

    def in_group(v):
        return lax.all_to_all(v, ("row", "col"), 0, 0, tiled=True, axis_index_groups=[[group[n] for n in order] for group in groups])

    def gathered(v):
        v = v[None]
        for bit in COL_BITS:
            other = lax.ppermute(v, "col", [(c, c ^ bit) for c in range(ncol)])
            upper = (lax.axis_index("col") & bit) == bit
            v = jnp.concatenate([jnp.where(upper, other, v), jnp.where(upper, v, other)])
        return v

    parts = turned(x).reshape(1, ratio, rb, b)
    got = in_group(jnp.broadcast_to(parts, (ncol, ratio, rb, b)).reshape(nrow, rb, b))
    xr = jnp.einsum("sb,nbl->nsl", pick(rows, rb), got, preferred_element_type=jnp.float32).astype(BF)

    prod = jnp.einsum("nki,kij->nkj", xr, local, preferred_element_type=jnp.float32).astype(BF)
    tail = jnp.zeros((8, b), BF).at[0, :k].set(cols.astype(BF)).at[1, :k].set(rows.astype(BF))
    got = exchange(jnp.concatenate([prod, jnp.broadcast_to(tail[None], (nrow, 8, b))], axis=1))
    named = jnp.pad(got[:, k, :k].astype(jnp.int32), ((0, 0), (0, 8)), constant_values=-1)
    pick_c = pick(named, cb)
    pick_r = pick(got[:, k + 1, :k].astype(jnp.int32), rb).reshape(nrow, k, rb)
    total = lax.dot_general(
        pick_c, got.reshape(nrow * (k + 8), b), (((0,), (0,)), ((), ())), preferred_element_type=jnp.float32
    )
    xf = x.astype(jnp.float32)
    mixed = (total + xf * diag).astype(BF)

    quad = (xf * mixed.astype(jnp.float32)).reshape(nrow, own, b)
    out = jnp.dot(pick_c, jnp.concatenate([mixed, x], axis=1), preferred_element_type=jnp.float32).astype(BF)
    out = out.reshape(nrow, k + 8, 2 * b)[:, :k]
    out = jnp.concatenate([out[..., :b], *halves(quad), out[..., b:]], axis=1)
    out, mixed = lax.optimization_barrier((out, mixed))
    got = exchange(out)

    held = gathered(mixed).reshape(nrow, rb, b)
    out = jnp.einsum("tsb,tbl->tsl", pick_r, held, preferred_element_type=jnp.float32).astype(BF)
    out, got = lax.optimization_barrier((out, got))

    wc, xc = got[:, :k], got[:, k + 2 * own :]
    quad = jnp.sum(got[:, k : k + 2 * own].astype(jnp.float32), axis=0)
    quad = quad[:own] + quad[own:]
    place = jnp.array([order.index(n) for n in range(nrow)], jnp.int32)[lax.axis_index("row")]
    mine = lax.dynamic_slice_in_dim(diag, place * own, own, 0)
    diag_grad = -1.0 / mine + quad / nrow
    mine = mine - TAU * diag_grad

    mine = jnp.concatenate(halves(mine))
    got = exchange(jnp.concatenate([out, jnp.broadcast_to(mine[None], (nrow, 2 * own, b))], axis=1))
    wr = got[:, :k]
    new_diagonal = got[:, k : k + own].astype(jnp.float32) + got[:, k + own :].astype(jnp.float32)

    left = jnp.concatenate([xr, wr], axis=0)
    right = jnp.concatenate([wc, xc], axis=0)
    both = jnp.einsum("nki,nkj->kij", left, right, preferred_element_type=jnp.float32)
    grad = both * (0.5 / nrow)
    moved = local.astype(jnp.float32) - TAU * grad
    shrunk = jnp.sign(moved) * jnp.maximum(jnp.abs(moved) - TAU * PENALTY, 0.0)
    return shrunk.astype(BF)[None, None], new_diagonal.reshape(width)


def solution(mesh):
    in_specs = (
        P("row", "col"),
        P("row", "col", None, None, None),
        P("col"),
        P("row", "col", None),
        P("row", "col", None),
    )
    out_specs = (P("row", "col", None, None, None), P("col"))
    return jax.shard_map(
        on_device, mesh=mesh, in_specs=in_specs, out_specs=out_specs, check_vma=False
    )
```

```python
import jax
import jax.numpy as jnp
from jax import lax
from jax.sharding import PartitionSpec as P

TAU = 0.5
PENALTY = 0.1
COL_BITS = (8, 2, 4, 1)
BF = jnp.bfloat16


def member_order():
    order = [0]
    for bit in COL_BITS:
        order = order + [c + bit for c in order]
    return [2 * c + e for c in order for e in range(2)]


def seats(ncol):
    def ring(a, b, size):
        return min((a - b) % size, (b - a) % size)

    def within(a, b):
        return ring(a // 4, b // 4, 4) + (2 if (a ^ b) & 2 else 0)

    out = []
    for g in range(ncol):
        planes = sorted(range(ncol), key=lambda m: (-ring(m, g, ncol), m))
        places = sorted(range(ncol), key=lambda c: (within(c, g), c))
        out.append([places[planes.index(m)] for m in range(ncol)])
    return out


def exchange(x):
    return lax.all_to_all(x, "row", 0, 0, tiled=True, axis_index_groups=[member_order()])


def pick(index, size):
    return (index.reshape(-1, 1) == jnp.arange(size, dtype=index.dtype)[None, :]).astype(BF)


def halves(v):
    high = lax.reduce_precision(v, 8, 7)
    return high.astype(BF), (v - high).astype(BF)


def on_device(samples, blocks, diagonal, block_rows, block_cols):
    nrow, ncol = lax.axis_size("row"), lax.axis_size("col")
    ratio = nrow // ncol
    width = samples.shape[1]
    b = blocks.shape[-1]
    cb = width // b
    rb = cb // ratio
    own = cb // nrow
    rows, cols, local = block_rows[0, 0], block_cols[0, 0], blocks[0, 0]
    k = rows.shape[0]
    x = samples.reshape(cb, b)
    diag = diagonal.reshape(cb, b)

    order = member_order()
    seat = seats(ncol)
    groups = [[(ratio * g + n % ratio) * ncol + seat[g][n // ratio] for n in range(nrow)] for g in range(ncol)]
    perm = [(n * ncol + g, groups[g][n]) for n in range(nrow) for g in range(ncol)]

    def turned(v):
        return lax.ppermute(v, ("row", "col"), perm)

    def in_group(v):
        return lax.all_to_all(v, ("row", "col"), 0, 0, tiled=True, axis_index_groups=[[group[n] for n in order] for group in groups])

    def gathered(v):
        v = v[None]
        for bit in COL_BITS:
            other = lax.ppermute(v, "col", [(c, c ^ bit) for c in range(ncol)])
            upper = (lax.axis_index("col") & bit) == bit
            v = jnp.concatenate([jnp.where(upper, other, v), jnp.where(upper, v, other)])
        return v

    parts = turned(x).reshape(1, ratio, rb, b)
    got = in_group(jnp.broadcast_to(parts, (ncol, ratio, rb, b)).reshape(nrow, rb, b))
    xr = jnp.einsum("sb,nbl->nsl", pick(rows, rb), got, preferred_element_type=jnp.float32).astype(BF)

    prod = jnp.einsum("nki,kij->nkj", xr, local, preferred_element_type=jnp.float32).astype(BF)
    tail = jnp.zeros((8, b), BF).at[0, :k].set(cols.astype(BF)).at[1, :k].set(rows.astype(BF))
    got = exchange(jnp.concatenate([prod, jnp.broadcast_to(tail[None], (nrow, 8, b))], axis=1))
    named = jnp.pad(got[:, k, :k].astype(jnp.int32), ((0, 0), (0, 8)), constant_values=-1)
    pick_c = pick(named, cb)
    pick_r = pick(got[:, k + 1, :k].astype(jnp.int32), rb).reshape(nrow, k, rb)
    total = lax.dot_general(
        pick_c, got.reshape(nrow * (k + 8), b), (((0,), (0,)), ((), ())), preferred_element_type=jnp.float32
    )
    xf = x.astype(jnp.float32)
    mixed = (total + xf * diag).astype(BF)

    quad = (xf * mixed.astype(jnp.float32)).reshape(nrow, own, b)
    out = jnp.dot(pick_c, jnp.concatenate([mixed, x], axis=1), preferred_element_type=jnp.float32).astype(BF)
    out = out.reshape(nrow, k + 8, 2 * b)[:, :k]
    out = jnp.concatenate([out[..., :b], *halves(quad), out[..., b:]], axis=1)
    out, mixed = lax.optimization_barrier((out, mixed))
    got = exchange(out)

    held = gathered(mixed).reshape(nrow, rb, b)
    out = jnp.einsum("tsb,tbl->tsl", pick_r, held, preferred_element_type=jnp.float32).astype(BF)
    out, got = lax.optimization_barrier((out, got))

    wc, xc = got[:, :k], got[:, k + 2 * own :]
    quad = jnp.sum(got[:, k : k + 2 * own].astype(jnp.float32), axis=0)
    quad = quad[:own] + quad[own:]
    place = jnp.array([order.index(n) for n in range(nrow)], jnp.int32)[lax.axis_index("row")]
    mine = lax.dynamic_slice_in_dim(diag, place * own, own, 0)
    diag_grad = -1.0 / mine + quad / nrow
    mine = mine - TAU * diag_grad

    mine = jnp.concatenate(halves(mine))
    got = exchange(jnp.concatenate([out, jnp.broadcast_to(mine[None], (nrow, 2 * own, b))], axis=1))
    wr = got[:, :k]
    new_diagonal = got[:, k : k + own].astype(jnp.float32) + got[:, k + own :].astype(jnp.float32)

    left = jnp.concatenate([xr, wr], axis=0)
    right = jnp.concatenate([wc, xc], axis=0)
    both = jnp.einsum("nki,nkj->kij", left, right, preferred_element_type=jnp.float32)
    grad = both * (0.5 / nrow)
    moved = local.astype(jnp.float32) - TAU * grad
    shrunk = jnp.sign(moved) * jnp.maximum(jnp.abs(moved) - TAU * PENALTY, 0.0)
    return shrunk.astype(BF)[None, None], new_diagonal.reshape(width)


def solution(mesh):
    in_specs = (
        P("row", "col"),
        P("row", "col", None, None, None),
        P("col"),
        P("row", "col", None),
        P("row", "col", None),
    )
    out_specs = (P("row", "col", None, None, None), P("col"))
    return jax.shard_map(
        on_device, mesh=mesh, in_specs=in_specs, out_specs=out_specs, check_vma=False
    )
```

```python
import jax
import jax.numpy as jnp
from jax import lax
from jax.sharding import PartitionSpec as P

TAU = 0.5
PENALTY = 0.1
COL_BITS = (8, 2, 4, 1)
BF = jnp.bfloat16


def member_order():
    order = [0]
    for bit in COL_BITS:
        order = order + [c + bit for c in order]
    return [2 * c + e for c in order for e in range(2)]


def seats(ncol):
    def ring(a, b, size):
        return min((a - b) % size, (b - a) % size)

    def within(a, b):
        return ring(a // 4, b // 4, 4) + (2 if (a ^ b) & 2 else 0)

    out = []
    for g in range(ncol):
        planes = sorted(range(ncol), key=lambda m: (-ring(m, g, ncol), m))
        places = sorted(range(ncol), key=lambda c: (within(c, g), c))
        out.append([places[planes.index(m)] for m in range(ncol)])
    return out


def exchange(x):
    return lax.all_to_all(x, "row", 0, 0, tiled=True, axis_index_groups=[member_order()])


def joined_exchange(*parts):
    parts = [part.reshape(part.shape[0], -1, 4, part.shape[-1]) for part in parts]
    return exchange(jnp.concatenate(parts, axis=1))


def pick(index, size):
    return (index.reshape(-1, 1) == jnp.arange(size, dtype=index.dtype)[None, :]).astype(BF)


def on_device(samples, blocks, diagonal, block_rows, block_cols):
    nrow, ncol = lax.axis_size("row"), lax.axis_size("col")
    ratio = nrow // ncol
    width = samples.shape[1]
    b = blocks.shape[-1]
    cb = width // b
    rb = cb // ratio
    own = cb // nrow
    rows, cols, local = block_rows[0, 0], block_cols[0, 0], blocks[0, 0]
    k = rows.shape[0]
    x = samples.reshape(cb, b)
    diag = diagonal.reshape(cb, b)

    order = member_order()
    seat = seats(ncol)
    groups = [[(ratio * g + n % ratio) * ncol + seat[g][n // ratio] for n in range(nrow)] for g in range(ncol)]
    perm = [(n * ncol + g, groups[g][n]) for n in range(nrow) for g in range(ncol)]

    def turned(v):
        return lax.ppermute(v, ("row", "col"), perm)

    def in_group(v):
        return lax.all_to_all(v, ("row", "col"), 0, 0, tiled=True, axis_index_groups=[[group[n] for n in order] for group in groups])

    def gathered(v):
        v = v[None]
        for bit in COL_BITS:
            other = lax.ppermute(v, "col", [(c, c ^ bit) for c in range(ncol)])
            upper = (lax.axis_index("col") & bit) == bit
            v = jnp.concatenate([jnp.where(upper, other, v), jnp.where(upper, v, other)])
        return v

    parts = turned(x).reshape(1, ratio, rb, b)
    got = in_group(jnp.broadcast_to(parts, (ncol, ratio, rb, b)).reshape(nrow, rb, b))
    xr = jnp.einsum("sb,nbl->nsl", pick(rows, rb), got, preferred_element_type=jnp.float32).astype(BF)

    prod = jnp.einsum("nki,kij->nkj", xr, local, preferred_element_type=jnp.float32).astype(BF)
    tail = jnp.zeros((4, b), BF).at[0, :k].set(cols.astype(BF)).at[1, :k].set(rows.astype(BF))
    got = joined_exchange(prod, jnp.broadcast_to(tail[None], (nrow, 4, b)))
    named = got[:, k // 4, :2, :k].astype(jnp.int32)
    spread = jnp.pad(named[:, 0], ((0, 0), (0, 4)), constant_values=-1)
    total = lax.dot_general(
        pick(spread, cb), got.reshape(nrow * (k + 4), b), (((0,), (0,)), ((), ())), preferred_element_type=jnp.float32
    )
    pick_c = pick(named[:, 0], cb)
    pick_r = pick(named[:, 1], rb).reshape(nrow, k, rb)
    xf = x.astype(jnp.float32)
    mixed = (total + xf * diag).astype(BF)

    quad = (xf * mixed.astype(jnp.float32)).reshape(nrow, own, b)
    out = jnp.dot(pick_c, jnp.concatenate([mixed, x], axis=1), preferred_element_type=jnp.float32).astype(BF)
    out = out.reshape(nrow, k, 2 * b)
    out, quad, mixed = lax.optimization_barrier((out, quad.astype(BF), mixed))
    got = joined_exchange(out[..., :b], quad, out[..., b:])

    held = gathered(mixed).reshape(nrow, rb, b)
    out = jnp.einsum("tsb,tbl->tsl", pick_r, held, preferred_element_type=jnp.float32).astype(BF)
    out, got = lax.optimization_barrier((out, got))

    wc, xc = got[:, : k // 4].reshape(nrow, k, b), got[:, -k // 4 :].reshape(nrow, k, b)
    quad = jnp.sum(got[:, k // 4 : -k // 4].astype(jnp.float32), axis=0).reshape(own, b).astype(BF)
    got = joined_exchange(out, jnp.broadcast_to(quad[None], (nrow, own, b)))
    wr = got[:, : k // 4].reshape(nrow, k, b)
    quad = got[:, k // 4 :].reshape(cb, b).astype(jnp.float32)
    diag_grad = -1.0 / diag + quad / nrow
    new_diagonal = diag - TAU * diag_grad

    left = jnp.concatenate([xr, wr], axis=0)
    right = jnp.concatenate([wc, xc], axis=0)
    both = jnp.einsum("nki,nkj->kij", left, right, preferred_element_type=jnp.float32)
    grad = both * (0.5 / nrow)
    moved = local.astype(jnp.float32) - TAU * grad
    shrunk = jnp.sign(moved) * jnp.maximum(jnp.abs(moved) - TAU * PENALTY, 0.0)
    return shrunk.astype(BF)[None, None], new_diagonal.reshape(width)


def solution(mesh):
    in_specs = (
        P("row", "col"),
        P("row", "col", None, None, None),
        P("col"),
        P("row", "col", None),
        P("row", "col", None),
    )
    out_specs = (P("row", "col", None, None, None), P("col"))
    return jax.shard_map(
        on_device, mesh=mesh, in_specs=in_specs, out_specs=out_specs, check_vma=False
    )
```

```python
import jax
import jax.numpy as jnp
from jax import lax
from jax.sharding import PartitionSpec as P

TAU = 0.5
PENALTY = 0.1
COL_BITS = (1, 8, 2, 4)
BF = jnp.bfloat16


def member_order():
    order = [0]
    for bit in COL_BITS:
        order = order + [c + bit for c in order]
    return [2 * c + e for c in order for e in range(2)]


def seats(ncol):
    def ring(a, b, size):
        return min((a - b) % size, (b - a) % size)

    def within(a, b):
        return ring(a // 4, b // 4, 4) + (2 if (a ^ b) & 2 else 0)

    out = []
    for g in range(ncol):
        planes = sorted(range(ncol), key=lambda m: (-ring(m, g, ncol), m))
        places = sorted(range(ncol), key=lambda c: (within(c, g), c))
        out.append([places[planes.index(m)] for m in range(ncol)])
    return out


def exchange(x):
    return lax.all_to_all(x, "row", 0, 0, tiled=True, axis_index_groups=[member_order()])


def joined_exchange(*parts):
    parts = [part.reshape(part.shape[0], -1, 4, part.shape[-1]) for part in parts]
    return exchange(jnp.concatenate(parts, axis=1))


def pick(index, size):
    return (index.reshape(-1, 1) == jnp.arange(size, dtype=index.dtype)[None, :]).astype(BF)


def on_device(samples, blocks, diagonal, block_rows, block_cols):
    nrow, ncol = lax.axis_size("row"), lax.axis_size("col")
    ratio = nrow // ncol
    width = samples.shape[1]
    b = blocks.shape[-1]
    cb = width // b
    rb = cb // ratio
    own = cb // nrow
    rows, cols, local = block_rows[0, 0], block_cols[0, 0], blocks[0, 0]
    k = rows.shape[0]
    x = samples.reshape(cb, b)
    diag = diagonal.reshape(cb, b)

    order = member_order()
    seat = seats(ncol)
    groups = [[(ratio * g + n % ratio) * ncol + seat[g][n // ratio] for n in range(nrow)] for g in range(ncol)]
    perm = [(n * ncol + g, groups[g][n]) for n in range(nrow) for g in range(ncol)]

    def turned(v):
        return lax.ppermute(v, ("row", "col"), perm)

    def in_group(v):
        return lax.all_to_all(v, ("row", "col"), 0, 0, tiled=True, axis_index_groups=[[group[n] for n in order] for group in groups])

    def gathered(v):
        v = v[None]
        for bit in COL_BITS:
            other = lax.ppermute(v, "col", [(c, c ^ bit) for c in range(ncol)])
            upper = (lax.axis_index("col") & bit) == bit
            v = jnp.concatenate([jnp.where(upper, other, v), jnp.where(upper, v, other)])
        return v

    parts = turned(x).reshape(1, ratio, rb, b)
    got = in_group(jnp.broadcast_to(parts, (ncol, ratio, rb, b)).reshape(nrow, rb, b))
    xr = jnp.einsum("sb,nbl->nsl", pick(rows, rb), got, preferred_element_type=jnp.float32).astype(BF)

    prod = jnp.einsum("nki,kij->nkj", xr, local, preferred_element_type=jnp.float32).astype(BF)
    tail = jnp.zeros((4, b), BF).at[0, :k].set(cols.astype(BF)).at[1, :k].set(rows.astype(BF))
    got = joined_exchange(prod, jnp.broadcast_to(tail[None], (nrow, 4, b)))
    named = got[:, k // 4, :2, :k].astype(jnp.int32)
    spread = jnp.pad(named[:, 0], ((0, 0), (0, 4)), constant_values=-1)
    total = lax.dot_general(
        pick(spread, cb), got.reshape(nrow * (k + 4), b), (((0,), (0,)), ((), ())), preferred_element_type=jnp.float32
    )
    pick_c = pick(named[:, 0], cb)
    pick_r = pick(named[:, 1], rb).reshape(nrow, k, rb)
    xf = x.astype(jnp.float32)
    mixed = (total + xf * diag).astype(BF)

    quad = (xf * mixed.astype(jnp.float32)).reshape(nrow, own, b)
    out = jnp.dot(pick_c, jnp.concatenate([mixed, x], axis=1), preferred_element_type=jnp.float32).astype(BF)
    out = out.reshape(nrow, k, 2 * b)
    out, quad, mixed = lax.optimization_barrier((out, quad.astype(BF), mixed))
    got = joined_exchange(out[..., :b], quad, out[..., b:])

    held = gathered(mixed).reshape(nrow, rb, b)
    out = jnp.einsum("tsb,tbl->tsl", pick_r, held, preferred_element_type=jnp.float32).astype(BF)
    out, got = lax.optimization_barrier((out, got))

    wc, xc = got[:, : k // 4].reshape(nrow, k, b), got[:, -k // 4 :].reshape(nrow, k, b)
    quad = jnp.sum(got[:, k // 4 : -k // 4].astype(jnp.float32), axis=0).reshape(own, b).astype(BF)
    got = joined_exchange(out, jnp.broadcast_to(quad[None], (nrow, own, b)))
    wr = got[:, : k // 4].reshape(nrow, k, b)
    quad = got[:, k // 4 :].reshape(cb, b).astype(jnp.float32)
    diag_grad = -1.0 / diag + quad / nrow
    new_diagonal = diag - TAU * diag_grad

    left = jnp.concatenate([xr, wr], axis=0)
    right = jnp.concatenate([wc, xc], axis=0)
    both = jnp.einsum("nki,nkj->kij", left, right, preferred_element_type=jnp.float32)
    grad = both * (0.5 / nrow)
    moved = local.astype(jnp.float32) - TAU * grad
    shrunk = jnp.sign(moved) * jnp.maximum(jnp.abs(moved) - TAU * PENALTY, 0.0)
    return shrunk.astype(BF)[None, None], new_diagonal.reshape(width)


def solution(mesh):
    in_specs = (
        P("row", "col"),
        P("row", "col", None, None, None),
        P("col"),
        P("row", "col", None),
        P("row", "col", None),
    )
    out_specs = (P("row", "col", None, None, None), P("col"))
    return jax.shard_map(
        on_device, mesh=mesh, in_specs=in_specs, out_specs=out_specs, check_vma=False
    )
```

```python
import jax
import jax.numpy as jnp
from jax import lax
from jax.sharding import PartitionSpec as P

TAU = 0.5
PENALTY = 0.1
COL_BITS = (1, 8, 2, 4)
BF = jnp.bfloat16


def member_order():
    order = [0]
    for bit in COL_BITS:
        order = order + [c + bit for c in order]
    return [2 * c + e for c in order for e in range(2)]


def seats(ncol):
    def ring(a, b, size):
        return min((a - b) % size, (b - a) % size)

    def within(a, b):
        return ring(a // 4, b // 4, 4) + (2 if (a ^ b) & 2 else 0)

    out = []
    for g in range(ncol):
        planes = sorted(range(ncol), key=lambda m: (-ring(m, g, ncol), m))
        places = sorted(range(ncol), key=lambda c: (within(c, g), c))
        out.append([places[planes.index(m)] for m in range(ncol)])
    return out


def exchange(x):
    return lax.all_to_all(x, "row", 0, 0, tiled=True, axis_index_groups=[member_order()])


def joined_exchange(*parts):
    parts = [part.reshape(part.shape[0], -1, 4, part.shape[-1]) for part in parts]
    return exchange(jnp.concatenate(parts, axis=1))


def pick(index, size):
    return (index.reshape(-1, 1) == jnp.arange(size, dtype=index.dtype)[None, :]).astype(BF)


def on_device(samples, blocks, diagonal, block_rows, block_cols):
    nrow, ncol = lax.axis_size("row"), lax.axis_size("col")
    ratio = nrow // ncol
    width = samples.shape[1]
    b = blocks.shape[-1]
    cb = width // b
    rb = cb // ratio
    own = cb // nrow
    rows, cols, local = block_rows[0, 0], block_cols[0, 0], blocks[0, 0]
    k = rows.shape[0]
    x = samples.reshape(cb, b)
    diag = diagonal.reshape(cb, b)

    order = member_order()
    seat = seats(ncol)
    groups = [[(ratio * g + n % ratio) * ncol + seat[g][n // ratio] for n in range(nrow)] for g in range(ncol)]
    perm = [(n * ncol + g, groups[g][n]) for n in range(nrow) for g in range(ncol)]

    def turned(v):
        return lax.ppermute(v, ("row", "col"), perm)

    def in_group(v):
        return lax.all_to_all(v, ("row", "col"), 0, 0, tiled=True, axis_index_groups=[[group[n] for n in order] for group in groups])

    def gathered(v):
        v = v[None]
        for bit in COL_BITS:
            other = lax.ppermute(v, "col", [(c, c ^ bit) for c in range(ncol)])
            upper = (lax.axis_index("col") & bit) == bit
            v = jnp.concatenate([jnp.where(upper, other, v), jnp.where(upper, v, other)])
        return v

    parts = turned(x).reshape(1, ratio, rb, b)
    got = in_group(jnp.broadcast_to(parts, (ncol, ratio, rb, b)).reshape(nrow, rb, b))
    xr = jnp.einsum("sb,nbl->nsl", pick(rows, rb), got, preferred_element_type=jnp.float32).astype(BF)

    prod = jnp.einsum("nki,kij->nkj", xr, local, preferred_element_type=jnp.float32).astype(BF)
    tail = jnp.zeros((4, b), BF).at[0, :k].set(cols.astype(BF)).at[1, :k].set(rows.astype(BF))
    got = joined_exchange(prod, jnp.broadcast_to(tail[None], (nrow, 4, b)))
    named = got[:, k // 4, :2, :k].astype(jnp.int32)
    spread = jnp.pad(named[:, 0], ((0, 0), (0, 4)), constant_values=-1)
    total = lax.dot_general(
        pick(spread, cb), got.reshape(nrow * (k + 4), b), (((0,), (0,)), ((), ())), preferred_element_type=jnp.float32
    )
    pick_c = pick(named[:, 0], cb)
    pick_r = pick(named[:, 1], rb).reshape(nrow, k, rb)
    xf = x.astype(jnp.float32)
    mixed = (total + xf * diag).astype(BF)

    quad = (xf * mixed.astype(jnp.float32)).reshape(nrow, own, b)
    out = jnp.dot(pick_c, jnp.concatenate([mixed, x], axis=1), preferred_element_type=jnp.float32).astype(BF)
    out = out.reshape(nrow, k, 2 * b)
    out, quad, mixed = lax.optimization_barrier((out, quad.astype(BF), mixed))
    got = joined_exchange(out[..., :b], quad, out[..., b:])

    held = gathered(mixed).reshape(nrow, rb, b)
    out = jnp.einsum("tsb,tbl->tsl", pick_r, held, preferred_element_type=jnp.float32).astype(BF)

    wc, xc = got[:, : k // 4].reshape(nrow, k, b), got[:, -k // 4 :].reshape(nrow, k, b)
    quad = jnp.sum(got[:, k // 4 : -k // 4].astype(jnp.float32), axis=0).reshape(own, b).astype(BF)
    got = joined_exchange(out, jnp.broadcast_to(quad[None], (nrow, own, b)))
    wr = got[:, : k // 4].reshape(nrow, k, b)
    quad = got[:, k // 4 :].reshape(cb, b).astype(jnp.float32)
    diag_grad = -1.0 / diag + quad / nrow
    new_diagonal = diag - TAU * diag_grad

    left = jnp.concatenate([xr, wr], axis=0)
    right = jnp.concatenate([wc, xc], axis=0)
    both = jnp.einsum("nki,nkj->kij", left, right, preferred_element_type=jnp.float32)
    grad = both * (0.5 / nrow)
    moved = local.astype(jnp.float32) - TAU * grad
    shrunk = jnp.sign(moved) * jnp.maximum(jnp.abs(moved) - TAU * PENALTY, 0.0)
    return shrunk.astype(BF)[None, None], new_diagonal.reshape(width)


def solution(mesh):
    in_specs = (
        P("row", "col"),
        P("row", "col", None, None, None),
        P("col"),
        P("row", "col", None),
        P("row", "col", None),
    )
    out_specs = (P("row", "col", None, None, None), P("col"))
    return jax.shard_map(
        on_device, mesh=mesh, in_specs=in_specs, out_specs=out_specs, check_vma=False
    )
```

```python
import jax
import jax.numpy as jnp
from jax import lax
from jax.sharding import PartitionSpec as P

TAU = 0.5
PENALTY = 0.1
COL_BITS = (1, 8, 2, 4)
BF = jnp.bfloat16


def member_order():
    order = [0]
    for bit in COL_BITS:
        order = order + [c + bit for c in order]
    return [2 * c + e for c in order for e in range(2)]


def seats(ncol):
    def ring(a, b, size):
        return min((a - b) % size, (b - a) % size)

    def within(a, b):
        return ring(a // 4, b // 4, 4) + (2 if (a ^ b) & 2 else 0)

    out = []
    for g in range(ncol):
        planes = sorted(range(ncol), key=lambda m: (-ring(m, g, ncol), m))
        places = sorted(range(ncol), key=lambda c: (within(c, g), c))
        out.append([places[planes.index(m)] for m in range(ncol)])
    return out


def exchange(x):
    return lax.all_to_all(x, "row", 0, 0, tiled=True, axis_index_groups=[member_order()])


def joined_exchange(*parts):
    parts = [part.reshape(part.shape[0], -1, 4, part.shape[-1]) for part in parts]
    return exchange(jnp.concatenate(parts, axis=1))


def pick(index, size):
    return (index.reshape(-1, 1) == jnp.arange(size, dtype=index.dtype)[None, :]).astype(BF)


def on_device(samples, blocks, diagonal, block_rows, block_cols):
    nrow, ncol = lax.axis_size("row"), lax.axis_size("col")
    ratio = nrow // ncol
    width = samples.shape[1]
    b = blocks.shape[-1]
    cb = width // b
    rb = cb // ratio
    own = cb // nrow
    rows, cols, local = block_rows[0, 0], block_cols[0, 0], blocks[0, 0]
    k = rows.shape[0]
    x = samples.reshape(cb, b)
    diag = diagonal.reshape(cb, b)

    order = member_order()
    seat = seats(ncol)
    groups = [[(ratio * g + n % ratio) * ncol + seat[g][n // ratio] for n in range(nrow)] for g in range(ncol)]
    perm = [(n * ncol + g, groups[g][n]) for n in range(nrow) for g in range(ncol)]

    def turned(v):
        return lax.ppermute(v, ("row", "col"), perm)

    def in_group(v):
        return lax.all_to_all(v, ("row", "col"), 0, 0, tiled=True, axis_index_groups=[[group[n] for n in order] for group in groups])

    def gathered(v):
        v = v[None]
        for bit in COL_BITS:
            other = lax.ppermute(v, "col", [(c, c ^ bit) for c in range(ncol)])
            upper = (lax.axis_index("col") & bit) == bit
            v = jnp.concatenate([jnp.where(upper, other, v), jnp.where(upper, v, other)])
        return v

    parts = turned(x).reshape(1, ratio, rb, b)
    got = in_group(jnp.broadcast_to(parts, (ncol, ratio, rb, b)).reshape(nrow, rb, b))
    xr = jnp.einsum("sb,nbl->nsl", pick(rows, rb), got, preferred_element_type=jnp.float32).astype(BF)

    prod = jnp.einsum("nki,kij->nkj", xr, local, preferred_element_type=jnp.float32).astype(BF)
    tail = jnp.zeros((4, b), BF).at[0, :k].set(cols.astype(BF)).at[1, :k].set(rows.astype(BF))
    got = joined_exchange(prod, jnp.broadcast_to(tail[None], (nrow, 4, b)))
    named = got[:, k // 4, :2, :k].astype(jnp.int32)
    spread = jnp.pad(named[:, 0], ((0, 0), (0, 4)), constant_values=-1)
    total = lax.dot_general(
        pick(spread, cb), got.reshape(nrow * (k + 4), b), (((0,), (0,)), ((), ())), preferred_element_type=jnp.float32
    )
    pick_c = pick(named[:, 0], cb)
    pick_r = pick(named[:, 1], rb).reshape(nrow, k, rb)
    xf = x.astype(jnp.float32)
    mixed = (total + xf * diag).astype(BF)

    quad = (xf * mixed.astype(jnp.float32)).reshape(nrow, own, b)
    out = jnp.dot(pick_c, mixed, preferred_element_type=jnp.float32).astype(BF).reshape(nrow, k, b)
    side = jnp.dot(pick_c, x, preferred_element_type=jnp.float32).astype(BF).reshape(nrow, k, b)
    out, quad, mixed = lax.optimization_barrier((out, quad.astype(BF), mixed))
    got = joined_exchange(out, quad, side)

    held = gathered(mixed).reshape(nrow, rb, b)
    out = jnp.einsum("tsb,tbl->tsl", pick_r, held, preferred_element_type=jnp.float32).astype(BF)

    wc, xc = got[:, : k // 4].reshape(nrow, k, b), got[:, -k // 4 :].reshape(nrow, k, b)
    quad = jnp.sum(got[:, k // 4 : -k // 4].astype(jnp.float32), axis=0).reshape(own, b).astype(BF)
    got = joined_exchange(out, jnp.broadcast_to(quad[None], (nrow, own, b)))
    wr = got[:, : k // 4].reshape(nrow, k, b)
    quad = got[:, k // 4 :].reshape(cb, b).astype(jnp.float32)
    diag_grad = -1.0 / diag + quad / nrow
    new_diagonal = diag - TAU * diag_grad

    left = jnp.concatenate([xr, wr], axis=0)
    right = jnp.concatenate([wc, xc], axis=0)
    both = jnp.einsum("nki,nkj->kij", left, right, preferred_element_type=jnp.float32)
    grad = both * (0.5 / nrow)
    moved = local.astype(jnp.float32) - TAU * grad
    shrunk = jnp.sign(moved) * jnp.maximum(jnp.abs(moved) - TAU * PENALTY, 0.0)
    return shrunk.astype(BF)[None, None], new_diagonal.reshape(width)


def solution(mesh):
    in_specs = (
        P("row", "col"),
        P("row", "col", None, None, None),
        P("col"),
        P("row", "col", None),
        P("row", "col", None),
    )
    out_specs = (P("row", "col", None, None, None), P("col"))
    return jax.shard_map(
        on_device, mesh=mesh, in_specs=in_specs, out_specs=out_specs, check_vma=False
    )
```
